32 devices in a mesh: rep: 2 (over y), wide: 2 (over core), narrow: 8 (over z, x).
Axes of the slice: x: 2, y: 2, z: 4, core: 2. Of those that a mesh axis runs over, the one named last changes fastest.
Arguments:
- queries: bfloat16 [8, 120, 4096], P(('rep', 'wide'), None, 'narrow'), parts along dimension 0, may hold values from -6 to 6
- layer_rows: bfloat16 [8, 120, 4096], P(('rep', 'wide'), None, 'narrow'), parts along dimension 0, may hold values from -6 to 6
- positions: int32 [8, 120], P(('rep', 'wide')), parts along dimension 0, may hold values from 0 to 2047, as said below
- counts: int32 [8], P('rep'), parts along dimension 0, may hold values from 1 to 120, 300 in all
- key_cache: bfloat16 [8, 65536, 128], P(('rep', 'wide'), 'narrow'), parts along dimension 0, may hold values from -400 to 400
- value_cache: bfloat16 [8, 65536, 128], P(('rep', 'wide'), 'narrow'), parts along dimension 0, may hold values from -6 to 6
- out_weight: bfloat16 [4096, 4096], P(None, 'narrow'), may hold values from -0.09375 to 0.09375
- ffn_gain: bfloat16 [4096], replicated, may hold values from 0.5 to 2
- w_gate: bfloat16 [12288, 4096], P('narrow'), may hold values from -0.09375 to 0.09375
- w_up: bfloat16 [12288, 4096], P('narrow'), may hold values from -0.09375 to 0.09375
- w_down: bfloat16 [4096, 12288], P('narrow'), may hold values from -0.0546875 to 0.0546875
Outputs:
- refreshed: bfloat16 [600, 4096], P(('rep', 'wide'), 'narrow'), parts along dimension 0
The draws below stay inside these ranges and needn't reach their ends.
There are 2 independent parts, one for each index of `rep`. The reference program is written for one: setup_inputs(seed, part) draws one part's arguments, and reference() takes and returns one part's arrays. A program takes and returns all parts, laid end to end along the dimension named above; an argument that names none is the same for every part. Nothing has to cross between parts.
Inputs may be any that keep to these rules, and one draw needn't show every extreme that they name: Within each canvas the 120 slot positions are distinct. The live slots of a canvas are its first counts slots. The counts are taken part by part: the 4 counts of each part sum to 150 times the number of wide groups, so an array that holds several parts sums to that once for each part.
All inputs are finite; a program needn't handle non-finite values.
Results may differ from the reference program's by a relative error of at most 0.012.
The reference program's roundings to bfloat16 on the way (of `rotated`, `weights`, `attended`, `residual`, `balanced`, `normed` and `activated`) count: a program that leaves them out, or rounds other values in their place, can miss the bound.
Values may be sent and summed in bfloat16 or wider, within the bound.
A program may use at most 128 MiB of HBM per device.

```python
import math
import jax
import jax.numpy as jnp
import numpy as np
from jax import lax

D = 4096
FF = 12288
HEAD = 128
LEN = 2048
RCAP = 120
NC = 4
BAL = 150
N_WIDE = 2


def draw_positions(key, part):
    canvas_keys = jax.random.split(key, NC)

    def one_canvas(canvas_key):
        order_key, spot_key = jax.random.split(canvas_key)
        shuffled = jax.random.permutation(order_key, LEN)[:RCAP]
        lifted = jax.random.randint(spot_key, (), 0, RCAP)
        offset = LEN - 1 - shuffled[lifted]
        return ((shuffled + offset) % LEN).astype(jnp.int32)
    return jax.vmap(one_canvas)(canvas_keys)


def draw_key_cache(key, part):
    head_count = D // HEAD
    values = jnp.clip(jax.random.normal(key, (NC, head_count * LEN, HEAD), jnp.float32), -6.0, 6.0) * 2.5
    return values.astype(jnp.bfloat16)


def shard_levels(rng, shape, cuts, low, high):
    loudness, own = 1.0, jax.random.fold_in(rng, 6)
    for axis_at, blocks in cuts:
        heights = jnp.exp(jax.random.uniform(jax.random.fold_in(own, axis_at), (blocks,), jnp.float32, low / len(cuts), high / len(cuts)))
        loudness = loudness * jnp.repeat(heights, shape[axis_at] // blocks).reshape([-1 if axis == axis_at else 1 for axis in range(len(shape))])
    return loudness


def split_up(amount, total, most, slope):
    weights = [(1 << 20) // math.isqrt(standing ** slope) + 1 for standing in range(2, amount + 1)]
    surplus, holding = total - most - (amount - 1), [1] * (amount - 1)
    while surplus > 0:
        free = [i for i in range(amount - 1) if holding[i] < most]
        mass, remaining = sum([weights[i] for i in free]), surplus
        for i in free:
            more = min(most - holding[i], max(1, remaining * weights[i] // mass), surplus)
            holding[i] = holding[i] + more
            surplus = surplus - more
    return np.array([most] + holding)


def ragged_sizes(stream_key, number_of, total, most, lean):
    if number_of == 2:
        one = jax.random.randint(stream_key, (), max(1, total - most), min(most, total - 1) + 1)
        return jnp.stack([one, total - one])
    tallies = jnp.asarray(split_up(number_of, total, most, lean), jnp.int32)
    pairs = (number_of - 1) // 2
    donor, taker = tallies[1:1 + 2 * pairs:2], tallies[2:2 + 2 * pairs:2]
    slack = jnp.minimum(donor - 1, most - taker)
    shifted = jax.random.randint(jax.random.fold_in(stream_key, 1), (pairs,), 0, 1 << 20) % (slack + 1)
    tallies = tallies.at[1:1 + 2 * pairs:2].set(donor - shifted).at[2:2 + 2 * pairs:2].set(taker + shifted)
    return tallies[jax.random.permutation(jax.random.fold_in(stream_key, 2), number_of)]


def noise(own_key, extent, deviation, bound, cuts=(), kind=jnp.bfloat16):
    gain = shard_levels(own_key, extent, cuts, -0.22, 0.18) if cuts else 1.0
    result = jax.random.normal(own_key, extent, jnp.float32) * deviation * gain
    return jnp.minimum(jnp.maximum(result, -bound), bound).astype(kind)


def setup_inputs(seed: int = 0, part: int = 0) -> dict:
    key_of = jax.random.split(jax.random.key(seed), 12)
    part_splits = jax.random.split(jax.random.fold_in(key_of[11], part), 12)
    queries = noise(part_splits[0], (NC, RCAP, D), 1.0, 6.0, ((0, 2), (2, 8)))
    layer_rows = noise(part_splits[1], (NC, RCAP, D), 1.0, 6.0, ((0, 2), (2, 8)))
    positions = draw_positions(jax.random.fold_in(jax.random.fold_in(key_of[11], part), 71), part)
    counts = ragged_sizes(part_splits[3], NC, N_WIDE * BAL, RCAP, 2).astype(jnp.int32)
    key_cache = draw_key_cache(jax.random.fold_in(jax.random.fold_in(key_of[11], part), 71), part)
    value_cache = noise(part_splits[5], (NC, (D // HEAD) * LEN, HEAD), 1.0, 6.0, ((0, 2), (1, 8)))
    out_weight = noise(key_of[6], (D, D), D ** -0.5, 0.09375, ((1, 8),))
    ffn_gain = jnp.clip(jnp.exp(jax.random.uniform(key_of[7], (D,), jnp.float32, math.log(0.5), math.log(2.0))), 0.5, 2.0).astype(jnp.bfloat16)
    w_gate = noise(key_of[8], (FF, D), D ** -0.5, 0.09375, ((0, 8),))
    w_up = noise(key_of[9], (FF, D), D ** -0.5, 0.09375, ((0, 8),))
    w_down = noise(key_of[10], (D, FF), FF ** -0.5, 0.0546875, ((0, 8),))
    return {"queries": queries, "layer_rows": layer_rows, "positions": positions, "counts": counts, "key_cache": key_cache, "value_cache": value_cache, "out_weight": out_weight, "ffn_gain": ffn_gain, "w_gate": w_gate, "w_up": w_up, "w_down": w_down}


epsilon = 1e-05

def rotate_queries(queries_f32, positions):
    half_size = HEAD // 2
    frequency = 500000.0 ** (-2.0 * jnp.arange(half_size, dtype=jnp.float32) / HEAD)
    angles = positions.astype(jnp.float32)[..., None] * frequency
    cosine_table = jnp.cos(angles)[..., None, :]
    sine_table = jnp.sin(angles)[..., None, :]
    lower_half = queries_f32[..., :half_size]
    upper_half = queries_f32[..., half_size:]
    return jnp.concatenate([lower_half * cosine_table - upper_half * sine_table, upper_half * cosine_table + lower_half * sine_table], axis=-1)

def attend_canvas(inputs):
    query_rows, key_rows, value_rows = inputs
    head_count = D // HEAD
    key_heads = key_rows.astype(jnp.float32).reshape(head_count, LEN, HEAD)
    value_heads = value_rows.astype(jnp.float32).reshape(head_count, LEN, HEAD)
    query_heads = query_rows.astype(jnp.float32).reshape(RCAP, head_count, HEAD)
    scores = jnp.einsum('rhd,hpd->hrp', query_heads, key_heads) * HEAD ** (-0.5)
    row_peak = lax.optimization_barrier(jnp.max(scores, axis=2, keepdims=True))
    exponent = jnp.exp(scores - row_peak)
    totals = lax.optimization_barrier(jnp.sum(exponent, axis=2))
    weights = exponent.astype(jnp.bfloat16)
    mixture = jnp.einsum('hrp,hpd->rhd', weights.astype(jnp.float32), value_heads)
    attended = mixture / jnp.transpose(totals)[:, :, None]
    return attended.reshape(RCAP, D).astype(jnp.bfloat16)

def reference(queries, layer_rows, positions, counts, key_cache, value_cache, out_weight, ffn_gain, w_gate, w_up, w_down):
    head_count = D // HEAD
    canvas_count = queries.shape[0]
    rotated = rotate_queries(queries.astype(jnp.float32).reshape(canvas_count, RCAP, head_count, HEAD), positions)
    rotated = rotated.reshape(canvas_count, RCAP, D).astype(jnp.bfloat16)
    attended = lax.map(attend_canvas, (rotated, key_cache, value_cache))
    projected = jnp.dot(attended.reshape(-1, D), out_weight, preferred_element_type=jnp.float32)
    residual = (layer_rows.reshape(-1, D).astype(jnp.float32) + projected).astype(jnp.bfloat16)
    canvas_end = jnp.cumsum(counts, dtype=jnp.int32)
    canvas_start = canvas_end - counts
    global_slot = jnp.arange(N_WIDE * BAL, dtype=jnp.int32)
    canvas_of = lax.optimization_barrier(jnp.sum((canvas_end[None, :] <= global_slot[:, None]).astype(jnp.int32), axis=1, dtype=jnp.int32))
    within = global_slot - canvas_start[canvas_of]
    flat_slot = (canvas_of * RCAP + within).astype(jnp.int32)
    balanced = residual[flat_slot]
    balanced_f32 = balanced.astype(jnp.float32)
    normed = (balanced_f32 * lax.rsqrt(lax.optimization_barrier(jnp.mean(balanced_f32 * balanced_f32, axis=1, keepdims=True)) + epsilon) * ffn_gain.astype(jnp.float32)).astype(jnp.bfloat16)
    gate_sum = jnp.dot(normed, w_gate.T, preferred_element_type=jnp.float32)
    up_sum = jnp.dot(normed, w_up.T, preferred_element_type=jnp.float32)
    activated = (jax.nn.silu(gate_sum) * up_sum).astype(jnp.bfloat16)
    refreshed = (balanced_f32 + jnp.dot(activated, w_down.T, preferred_element_type=jnp.float32)).astype(jnp.bfloat16)
    return refreshed
```

```python
import functools

import jax
import jax.numpy as jnp
from jax import lax
from jax.experimental import pallas as pl
from jax.experimental.pallas import tpu as pltpu
from jax.sharding import PartitionSpec as P

D = 4096
HEAD = 128
BAL = 150
MESH = pl.DeviceIdType.MESH


epsilon = 1e-05


def from_partner(x, axis, distance):
    return lax.ppermute(x, axis, [(i, i ^ 1 << distance) for i in range(lax.axis_size(axis))])


def rotate_queries(queries_f32, positions):
    half_size = HEAD // 2
    frequency = 500000.0 ** (-2.0 * jnp.arange(half_size, dtype=jnp.float32) / HEAD)
    angles = positions.astype(jnp.float32)[..., None] * frequency
    cosine_table = jnp.cos(angles)[..., None, :]
    sine_table = jnp.sin(angles)[..., None, :]
    lower_half = queries_f32[..., :half_size]
    upper_half = queries_f32[..., half_size:]
    return jnp.concatenate(
        [
            lower_half * cosine_table - upper_half * sine_table,
            upper_half * cosine_table + lower_half * sine_table,
        ],
        axis=-1,
    )


def prefix_sum(counts):
    index = jnp.arange(counts.shape[0], dtype=jnp.int32)
    return jnp.sum(
        jnp.where(index[None, :] <= index[:, None], counts[None, :], 0), axis=1, dtype=jnp.int32
    )


def balanced_slots(counts, canvases, slot_cap, groups, share):
    canvas_total = counts.shape[0]
    canvas_end = prefix_sum(counts)
    canvas_start = canvas_end - counts
    global_slot = jnp.arange(groups * share, dtype=jnp.int32)
    canvas_of = jnp.sum(
        (canvas_end[None, :] <= global_slot[:, None]).astype(jnp.int32), axis=1, dtype=jnp.int32
    )
    canvas_of = jnp.minimum(canvas_of, canvas_total - 1)
    matches = canvas_of[:, None] == jnp.arange(canvas_total, dtype=jnp.int32)[None, :]
    picked_start = jnp.sum(jnp.where(matches, canvas_start[None, :], 0), axis=1, dtype=jnp.int32)
    within = global_slot - picked_start
    source = canvas_of // canvases
    local_slot = canvas_of % canvases * slot_cap + within
    return (source.reshape(groups, share), local_slot.reshape(groups, share))


def route_rows(rows_local, counts, canvases, slot_cap, groups, share):
    source, local_slot = balanced_slots(counts, canvases, slot_cap, groups, share)
    from_here = source == lax.axis_index("wide")
    picked = jnp.take(rows_local, jnp.where(from_here, local_slot, 0).reshape(-1), axis=0)
    picked = picked.reshape(groups, share, rows_local.shape[1])
    return jnp.where(from_here[:, :, None], picked, jnp.zeros_like(picked))


def feed_forward(residual, ffn_gain, w_gate, w_up, w_down):
    gathered = lax.all_gather(residual, "narrow", axis=1, tiled=True).astype(jnp.float32)
    normed = (
        gathered
        * lax.rsqrt(jnp.mean(gathered * gathered, axis=1, keepdims=True) + epsilon)
        * ffn_gain.astype(jnp.float32)
    ).astype(jnp.bfloat16)
    contract = (((1,), (1,)), ((), ()))
    gate_sum = lax.dot_general(normed, w_gate, contract, preferred_element_type=jnp.float32)
    up_sum = lax.dot_general(normed, w_up, contract, preferred_element_type=jnp.float32)
    activated = (jax.nn.silu(gate_sum) * up_sum).astype(jnp.bfloat16)
    output = lax.dot_general(
        lax.all_gather(activated, "narrow", axis=1, tiled=True),
        w_down,
        contract,
        preferred_element_type=jnp.float32,
    )
    return (residual.astype(jnp.float32) + output).astype(jnp.bfloat16)


def dot(a, b):
    return jnp.dot(a, b, preferred_element_type=jnp.float32)


def dot_t(a, b):
    return lax.dot_general(a, b, (((1,), (1,)), ((), ())), preferred_element_type=jnp.float32)


def rest_kernel(
    levels,
    chunks,
    att_ref,
    rows_ref,
    pick_ref,
    gain_ref,
    wo_hbm,
    wg_hbm,
    wu_hbm,
    wd_hbm,
    out_ref,
    wo,
    wg,
    wu,
    wd,
    other_att,
    other_rows,
    att_all,
    bal_all,
    act_all,
    gate_acc,
    up_acc,
    out_acc,
    w_sem,
    swap_send,
    swap_recv,
    a_send,
    a_recv,
    b_send,
    b_recv,
    c_send,
    c_recv,
):
    me = lax.axis_index("narrow")
    wide = lax.axis_index("wide")
    z, x = me // 2, me % 2
    far = z // (levels // 2)
    mirrored = z * (1 - far) + (levels - 1 - z) * far
    width = att_ref.shape[1]
    hidden = wg.shape[0]
    chunk = hidden // chunks

    loads = [
        pltpu.make_async_copy(src, dst, w_sem.at[i])
        for i, (src, dst) in enumerate(((wo_hbm, wo), (wg_hbm, wg), (wu_hbm, wu), (wd_hbm, wd)))
    ]
    for load in loads:
        load.start()

    barrier = pltpu.get_barrier_semaphore()

    def greet(axis, index):
        pl.semaphore_signal(barrier, inc=1, device_id={axis: index}, device_id_type=MESH)

    greet("wide", 1 - wide)
    greet("narrow", 2 * z + 1 - x)
    pl.when(z < levels - 1)(lambda: greet("narrow", me + 2))
    pl.when(z > 0)(lambda: greet("narrow", me - 2))
    pl.semaphore_wait(barrier, 3 + (z + levels - 2) // (levels - 1) - z // (levels - 1))

    swaps = [
        pltpu.make_async_remote_copy(
            src_ref=src,
            dst_ref=dst,
            send_sem=swap_send.at[i],
            recv_sem=swap_recv.at[i],
            device_id={"wide": 1 - wide},
            device_id_type=MESH,
        )
        for i, (src, dst) in enumerate(((att_ref, other_att), (rows_ref, other_rows)))
    ]
    for swap in swaps:
        swap.start()

    def column(k):
        if k == 0:
            return z
        near = 1 - mirrored if k == 1 else k
        return near * (1 - far) + (levels - 1 - near) * far

    sent = []

    def spread(ref, send, recv, k, c):
        level = column(k)
        slot = 2 * level + x

        def copy(way, target):
            return pltpu.make_async_remote_copy(
                src_ref=ref.at[slot, c],
                dst_ref=ref.at[slot, c],
                send_sem=send.at[k, c, way],
                recv_sem=recv.at[slot, c],
                device_id={"narrow": target},
                device_id_type=MESH,
            )

        across, up, down = copy(0, 2 * z + 1 - x), copy(1, me + 2), copy(2, me - 2)
        go_up = jnp.logical_and(level <= z, z < levels - 1)
        go_down = jnp.logical_and(level >= z, z > 0)
        pl.when(go_up)(up.start)
        pl.when(go_down)(down.start)
        across.start()
        sent.extend(((go_up, up), (go_down, down), (None, across)))

    def arrive(ref, recv, slot, c):
        pltpu.make_async_copy(ref.at[slot, c], ref.at[slot, c], recv.at[slot, c]).wait()

    def gather(ref, send, recv, pieces, use, own_sent=False):
        if not own_sent:
            for c in range(pieces):
                spread(ref, send, recv, 0, c)
        for c in range(pieces):
            use(me, c, c == 0)
        order = [(1, 0), (0, 1)]
        for k in range(2, levels):
            order += [(k, 0), (k - 1, 1)]
        order += [(levels - 1, 1)]
        for k, other in order:
            slot = 2 * column(k) + (1 - x if other else x)
            for c in range(pieces):
                arrive(ref, recv, slot, c)
                if not other:
                    spread(ref, send, recv, k, c)
                use(slot, c, False)

    def picked(mine, theirs):
        return dot(pick_ref[wide], mine[...]) + dot(pick_ref[1 - wide], theirs[...])

    swaps[0].wait()
    att_all[me, 0] = picked(att_ref, other_att).astype(jnp.bfloat16)

    def project(slot, c, first):
        part = dot(att_all[slot, c], wo[pl.ds(pl.multiple_of(slot * width, width), width), :])
        if first:
            swaps[1].wait()
            out_acc[...] = picked(rows_ref, other_rows) + part
        else:
            out_acc[...] += part

    spread(att_all, a_send, a_recv, 0, 0)
    loads[0].wait()
    gather(att_all, a_send, a_recv, 1, project, own_sent=True)

    balanced = out_acc[...].astype(jnp.bfloat16)
    bal_all[me, 0] = balanced
    spread(bal_all, b_send, b_recv, 0, 0)
    loads[1].wait()
    loads[2].wait()
    squares = []

    def expand(slot, c, first):
        block = bal_all[slot, c].astype(jnp.float32)
        squares.append(jnp.sum(block * block, axis=1, keepdims=True))
        columns = pl.ds(pl.multiple_of(slot * width, width), width)
        scaled = (block * gain_ref[:, columns].astype(jnp.float32)).astype(jnp.bfloat16)
        for j in range(chunks):
            part = pl.ds(j * chunk, chunk)
            gate = dot_t(scaled, wg[part, columns])
            up = dot_t(scaled, wu[part, columns])
            if first:
                gate_acc[:, part] = gate
                up_acc[:, part] = up
            else:
                gate_acc[:, part] += gate
                up_acc[:, part] += up

    gather(bal_all, b_send, b_recv, 1, expand, own_sent=True)

    scale = lax.rsqrt(sum(squares) / (width * 2 * levels) + epsilon)
    for c in range(chunks):
        part = pl.ds(c * chunk, chunk)
        gate = gate_acc[:, part] * scale
        up = up_acc[:, part] * scale
        act_all[me, c] = (gate / (1.0 + jnp.exp(-gate)) * up).astype(jnp.bfloat16)
        spread(act_all, c_send, c_recv, 0, c)

    out_acc[...] = bal_all[me, 0].astype(jnp.float32)
    loads[3].wait()

    def contract(slot, c, first):
        columns = pl.ds(pl.multiple_of(slot * hidden + c * chunk, chunk), chunk)
        out_acc[...] += dot_t(act_all[slot, c], wd[:, columns])

    gather(act_all, c_send, c_recv, chunks, contract, own_sent=True)
    out_ref[...] = out_acc[: out_ref.shape[0], :].astype(jnp.bfloat16)
    for condition, copy in sent:
        if condition is None:
            copy.wait_send()
        else:
            pl.when(condition)(copy.wait_send)


def rest(attended, layer_rows, counts, ffn_gain, out_weight, w_gate, w_up, w_down, slot_cap):
    groups, narrow_count = lax.axis_size("wide"), lax.axis_size("narrow")
    row_count, width = attended.shape
    hidden = w_gate.shape[0]
    levels = narrow_count // 2
    chunks = 3
    padded = -(-BAL // 16) * 16
    canvas_end = prefix_sum(counts)
    canvas_start = canvas_end - counts
    slots = jnp.arange(row_count * groups, dtype=jnp.int32)
    canvas = slots // slot_cap
    chosen = canvas[:, None] == jnp.arange(counts.shape[0], dtype=jnp.int32)[None, :]
    within = slots % slot_cap
    start = jnp.sum(jnp.where(chosen, canvas_start[None, :], 0), axis=1, dtype=jnp.int32)
    count = jnp.sum(jnp.where(chosen, counts[None, :], 0), axis=1, dtype=jnp.int32)
    place = jnp.where(within < count, start + within - lax.axis_index("wide") * BAL, -1)
    place = place.reshape(groups, 1, row_count)
    target = jnp.arange(padded, dtype=jnp.int32)[None, :, None]
    pick = jnp.logical_and(place == target, target < BAL).astype(jnp.bfloat16)

    vmem = pl.BlockSpec(memory_space=pltpu.VMEM)
    hbm = pl.BlockSpec(memory_space=pl.ANY)
    chunk = hidden // chunks
    sems = pltpu.SemaphoreType.DMA
    return pl.pallas_call(
        functools.partial(rest_kernel, levels, chunks),
        out_shape=jax.ShapeDtypeStruct((BAL, width), jnp.bfloat16),
        in_specs=[vmem] * 4 + [hbm] * 4,
        out_specs=vmem,
        scratch_shapes=[
            pltpu.VMEM(out_weight.shape, jnp.bfloat16),
            pltpu.VMEM(w_gate.shape, jnp.bfloat16),
            pltpu.VMEM(w_up.shape, jnp.bfloat16),
            pltpu.VMEM(w_down.shape, jnp.bfloat16),
            pltpu.VMEM((row_count, width), jnp.bfloat16),
            pltpu.VMEM((row_count, width), jnp.bfloat16),
            pltpu.VMEM((narrow_count, 1, padded, width), jnp.bfloat16),
            pltpu.VMEM((narrow_count, 1, padded, width), jnp.bfloat16),
            pltpu.VMEM((narrow_count, chunks, padded, chunk), jnp.bfloat16),
            pltpu.VMEM((padded, hidden), jnp.float32),
            pltpu.VMEM((padded, hidden), jnp.float32),
            pltpu.VMEM((padded, width), jnp.float32),
            sems((4,)),
            sems((2,)),
            sems((2,)),
            sems((levels, 1, 3)),
            sems((narrow_count, 1)),
            sems((levels, 1, 3)),
            sems((narrow_count, 1)),
            sems((levels, chunks, 3)),
            sems((narrow_count, chunks)),
        ],
        compiler_params=pltpu.CompilerParams(
            collective_id=0, has_side_effects=True, vmem_limit_bytes=60 * 2**20
        ),
    )(attended, layer_rows, pick, ffn_gain.reshape(1, -1), out_weight, w_gate, w_up, w_down)


def fits_kernel(narrow_count, groups, width, hidden):
    return narrow_count == 8 and groups == 2 and width % 128 == 0 and hidden % 384 == 0


def per_device(
    queries,
    layer_rows,
    positions,
    counts,
    key_cache,
    value_cache,
    out_weight,
    ffn_gain,
    w_gate,
    w_up,
    w_down,
):
    canvases, slot_cap, feature_share = queries.shape
    head_count = D // HEAD
    narrow_count = lax.axis_size("narrow")
    groups = lax.axis_size("wide")
    row_count = canvases * slot_cap
    group_size = max(1, narrow_count // head_count)
    local_heads = max(1, head_count // narrow_count)
    bit_steps = group_size.bit_length() - 1
    device_index = lax.axis_index("narrow")
    joined = queries
    for level in range(bit_steps):
        partner = from_partner(joined, "narrow", level)
        upper_bit = device_index // 2**level % 2 == 1
        joined = jnp.where(
            upper_bit,
            jnp.concatenate([partner, joined], axis=2),
            jnp.concatenate([joined, partner], axis=2),
        )
    rotated = rotate_queries(
        joined.astype(jnp.float32).reshape(canvases, slot_cap, local_heads, HEAD), positions
    ).astype(jnp.bfloat16)
    block_rows = key_cache.shape[1] // local_heads
    key_blocks = key_cache.reshape(canvases, local_heads, block_rows, HEAD)
    value_blocks = value_cache.reshape(canvases, local_heads, block_rows, HEAD)
    scores = jnp.einsum(
        "crhd,chpd->chrp", rotated, key_blocks, preferred_element_type=jnp.float32
    ) * HEAD ** (-0.5)
    row_peak = jnp.max(scores, axis=3)
    for level in range(bit_steps):
        other_peak = from_partner(row_peak, "narrow", level)
        row_peak = jnp.maximum(row_peak, other_peak)
    exponent = jnp.exp(scores - row_peak[..., None])
    totals = jnp.sum(exponent, axis=3)
    mixture = jnp.einsum(
        "chrp,chpd->crhd",
        exponent.astype(jnp.bfloat16),
        value_blocks,
        preferred_element_type=jnp.float32,
    ).reshape(row_count, local_heads * HEAD)
    for level in reversed(range(bit_steps)):
        half_width = mixture.shape[1] // 2
        lower_part = mixture[:, :half_width]
        upper_part = mixture[:, half_width:]
        upper_bit = device_index // 2**level % 2 == 1
        outgoing = jnp.where(upper_bit, lower_part, upper_part)
        kept = jnp.where(upper_bit, upper_part, lower_part)
        arrived, arrived_totals = from_partner((outgoing, totals), "narrow", level)
        mixture = kept + arrived
        totals = totals + arrived_totals
    divisor = jnp.repeat(
        jnp.transpose(totals, (0, 2, 1)).reshape(row_count, local_heads),
        mixture.shape[1] // local_heads,
        axis=1,
    )
    attended = (mixture / divisor).astype(jnp.bfloat16)
    if fits_kernel(narrow_count, groups, feature_share, w_gate.shape[0]):
        return rest(
            attended,
            layer_rows.reshape(row_count, feature_share),
            counts,
            ffn_gain,
            out_weight,
            w_gate,
            w_up,
            w_down,
            slot_cap,
        )
    projected = jnp.dot(
        lax.all_gather(attended, "narrow", axis=1, tiled=True),
        out_weight,
        preferred_element_type=jnp.float32,
    )
    residual = (
        layer_rows.reshape(row_count, feature_share).astype(jnp.float32) + projected
    ).astype(jnp.bfloat16)
    outgoing_rows = route_rows(residual, counts, canvases, slot_cap, groups, BAL)
    incoming = lax.all_to_all(outgoing_rows, "wide", split_axis=0, concat_axis=0, tiled=True)
    balanced = jnp.sum(incoming.astype(jnp.float32), axis=0).astype(jnp.bfloat16)
    return feed_forward(balanced, ffn_gain, w_gate, w_up, w_down)


def solution(mesh):
    return jax.shard_map(
        per_device,
        mesh=mesh,
        in_specs=(
            P(("rep", "wide"), None, "narrow"),
            P(("rep", "wide"), None, "narrow"),
            P(("rep", "wide"), None),
            P("rep"),
            P(("rep", "wide"), "narrow", None),
            P(("rep", "wide"), "narrow", None),
            P(None, "narrow"),
            P(),
            P("narrow", None),
            P("narrow", None),
            P("narrow", None),
        ),
        out_specs=P(("rep", "wide"), "narrow"),
        check_vma=False,
    )
```

```python
import functools

import jax
import jax.numpy as jnp
from jax import lax
from jax.experimental import pallas as pl
from jax.experimental.pallas import tpu as pltpu
from jax.sharding import PartitionSpec as P

D = 4096
HEAD = 128
BAL = 150
MESH = pl.DeviceIdType.MESH


epsilon = 1e-05


def from_partner(x, axis, distance):
    return lax.ppermute(x, axis, [(i, i ^ 1 << distance) for i in range(lax.axis_size(axis))])


def rotate_queries(queries_f32, positions):
    half_size = HEAD // 2
    frequency = 500000.0 ** (-2.0 * jnp.arange(half_size, dtype=jnp.float32) / HEAD)
    angles = positions.astype(jnp.float32)[..., None] * frequency
    cosine_table = jnp.cos(angles)[..., None, :]
    sine_table = jnp.sin(angles)[..., None, :]
    lower_half = queries_f32[..., :half_size]
    upper_half = queries_f32[..., half_size:]
    return jnp.concatenate(
        [
            lower_half * cosine_table - upper_half * sine_table,
            upper_half * cosine_table + lower_half * sine_table,
        ],
        axis=-1,
    )


def prefix_sum(counts):
    index = jnp.arange(counts.shape[0], dtype=jnp.int32)
    return jnp.sum(
        jnp.where(index[None, :] <= index[:, None], counts[None, :], 0), axis=1, dtype=jnp.int32
    )


def balanced_slots(counts, canvases, slot_cap, groups, share):
    canvas_total = counts.shape[0]
    canvas_end = prefix_sum(counts)
    canvas_start = canvas_end - counts
    global_slot = jnp.arange(groups * share, dtype=jnp.int32)
    canvas_of = jnp.sum(
        (canvas_end[None, :] <= global_slot[:, None]).astype(jnp.int32), axis=1, dtype=jnp.int32
    )
    canvas_of = jnp.minimum(canvas_of, canvas_total - 1)
    matches = canvas_of[:, None] == jnp.arange(canvas_total, dtype=jnp.int32)[None, :]
    picked_start = jnp.sum(jnp.where(matches, canvas_start[None, :], 0), axis=1, dtype=jnp.int32)
    within = global_slot - picked_start
    source = canvas_of // canvases
    local_slot = canvas_of % canvases * slot_cap + within
    return (source.reshape(groups, share), local_slot.reshape(groups, share))


def route_rows(rows_local, counts, canvases, slot_cap, groups, share):
    source, local_slot = balanced_slots(counts, canvases, slot_cap, groups, share)
    from_here = source == lax.axis_index("wide")
    picked = jnp.take(rows_local, jnp.where(from_here, local_slot, 0).reshape(-1), axis=0)
    picked = picked.reshape(groups, share, rows_local.shape[1])
    return jnp.where(from_here[:, :, None], picked, jnp.zeros_like(picked))


def feed_forward(residual, ffn_gain, w_gate, w_up, w_down):
    gathered = lax.all_gather(residual, "narrow", axis=1, tiled=True).astype(jnp.float32)
    normed = (
        gathered
        * lax.rsqrt(jnp.mean(gathered * gathered, axis=1, keepdims=True) + epsilon)
        * ffn_gain.astype(jnp.float32)
    ).astype(jnp.bfloat16)
    contract = (((1,), (1,)), ((), ()))
    gate_sum = lax.dot_general(normed, w_gate, contract, preferred_element_type=jnp.float32)
    up_sum = lax.dot_general(normed, w_up, contract, preferred_element_type=jnp.float32)
    activated = (jax.nn.silu(gate_sum) * up_sum).astype(jnp.bfloat16)
    output = lax.dot_general(
        lax.all_gather(activated, "narrow", axis=1, tiled=True),
        w_down,
        contract,
        preferred_element_type=jnp.float32,
    )
    return (residual.astype(jnp.float32) + output).astype(jnp.bfloat16)


def dot(a, b):
    return jnp.dot(a, b, preferred_element_type=jnp.float32)


def dot_t(a, b):
    return lax.dot_general(a, b, (((1,), (1,)), ((), ())), preferred_element_type=jnp.float32)


def rest_kernel(
    levels,
    chunks,
    slot_cap,
    counts_ref,
    att_ref,
    rows_ref,
    gain_ref,
    wo_hbm,
    wg_hbm,
    wu_hbm,
    wd_hbm,
    out_ref,
    wo,
    wg,
    wu,
    wd,
    other_att,
    other_rows,
    att_all,
    bal_all,
    act_all,
    gate_acc,
    up_acc,
    out_acc,
    w_sem,
    swap_send,
    swap_recv,
    a_send,
    a_recv,
    b_send,
    b_recv,
    c_send,
    c_recv,
):
    me = lax.axis_index("narrow")
    wide = lax.axis_index("wide")
    z, x = me // 2, me % 2
    far = z // (levels // 2)
    mirrored = z * (1 - far) + (levels - 1 - z) * far
    width = att_ref.shape[1]
    hidden = wg.shape[0]
    chunk = hidden // chunks

    loads = [
        pltpu.make_async_copy(src, dst, w_sem.at[i])
        for i, (src, dst) in enumerate(((wo_hbm, wo), (wg_hbm, wg), (wu_hbm, wu), (wd_hbm, wd)))
    ]
    loads[0].start()

    barrier = pltpu.get_barrier_semaphore()

    def greet(axis, index):
        pl.semaphore_signal(barrier, inc=1, device_id={axis: index}, device_id_type=MESH)

    greet("wide", 1 - wide)
    greet("narrow", 2 * z + 1 - x)
    pl.when(z < levels - 1)(lambda: greet("narrow", me + 2))
    pl.when(z > 0)(lambda: greet("narrow", me - 2))
    pl.semaphore_wait(barrier, 3 + (z + levels - 2) // (levels - 1) - z // (levels - 1))

    swaps = [
        pltpu.make_async_remote_copy(
            src_ref=src,
            dst_ref=dst,
            send_sem=swap_send.at[i],
            recv_sem=swap_recv.at[i],
            device_id={"wide": 1 - wide},
            device_id_type=MESH,
        )
        for i, (src, dst) in enumerate(((att_ref, other_att), (rows_ref, other_rows)))
    ]
    for swap in swaps:
        swap.start()

    def column(k):
        if k == 0:
            return z
        near = 1 - mirrored if k == 1 else k
        return near * (1 - far) + (levels - 1 - near) * far

    sent = []

    def spread(ref, send, recv, k, c, other, shared):
        level = column(k)
        slot = 2 * level + (1 - x if other else x)

        def copy(way, target):
            return pltpu.make_async_remote_copy(
                src_ref=ref.at[slot, c],
                dst_ref=ref.at[slot, c],
                send_sem=send.at[k, c, 3 * other + way],
                recv_sem=recv.at[slot, c],
                device_id={"narrow": target},
                device_id_type=MESH,
            )

        low, high = level == 0, level == levels - 1
        go_up, go_down = z < levels - 1, z > 0
        if other:
            go_up, go_down = go_up & low, go_down & high
        else:
            go_up, go_down = go_up & (level <= z), go_down & (level >= z)
        moves = [(go_up, copy(0, me + 2)), (go_down, copy(1, me - 2))]
        if not other:
            across = (level == z) | ((level > 0) & (level < levels - 1)) if shared else None
            moves.append((across, copy(2, 2 * z + 1 - x)))
        for condition, move in moves:
            if condition is None:
                move.start()
            else:
                pl.when(condition)(move.start)
        sent.extend(moves)

    def arrive(ref, recv, slot, c):
        pltpu.make_async_copy(ref.at[slot, c], ref.at[slot, c], recv.at[slot, c]).wait()

    def gather(ref, send, recv, pieces, use):
        for c in range(pieces):
            use(me, c, c == 0)
        order = [(1, 0), (0, 1)]
        for k in range(2, levels):
            order += [(k, 0), (k - 1, 1)]
        order += [(levels - 1, 1)]
        for k, other in order:
            slot = 2 * column(k) + (1 - x if other else x)
            for c in range(pieces):
                shared = c >= pieces // 2
                arrive(ref, recv, slot, c)
                if shared or not other:
                    spread(ref, send, recv, k, c, other, shared)
                use(slot, c, False)

    starts = [jnp.int32(0)]
    for i in range(counts_ref.shape[0] - 1):
        starts.append(starts[i] + counts_ref[i])
    canvases = att_ref.shape[0] // slot_cap
    shape = (out_acc.shape[0], att_ref.shape[0])
    row = lax.broadcasted_iota(jnp.int32, shape, 0) + wide * out_ref.shape[0]
    slot_index = lax.broadcasted_iota(jnp.int32, shape, 1)
    inside = lax.broadcasted_iota(jnp.int32, shape, 0) < out_ref.shape[0]

    def pick(group):
        found = jnp.zeros(shape, jnp.float32)
        for i in range(canvases):
            start = starts[i] * (1 - group) + starts[canvases + i] * group
            count = counts_ref[i] * (1 - group) + counts_ref[canvases + i] * group
            within = slot_index - i * slot_cap
            live = (within >= 0) & (within < slot_cap) & (within < count) & inside
            found += jnp.where(live & (start + within == row), 1.0, 0.0)
        return found.astype(jnp.bfloat16)

    pick_mine, pick_theirs = pick(wide), pick(1 - wide)

    def picked(mine, theirs):
        return dot(pick_mine, mine[...]) + dot(pick_theirs, theirs[...])

    half = att_all.shape[3]
    pieces = width // half

    def put(ref, send, recv, value):
        for c in range(pieces):
            ref[me, c] = value[:, c * half : (c + 1) * half]
            spread(ref, send, recv, 0, c, 0, c >= pieces // 2)

    swaps[0].wait()
    put(att_all, a_send, a_recv, picked(att_ref, other_att).astype(jnp.bfloat16))

    def project(slot, c, first):
        depth = pl.ds(pl.multiple_of(slot * width + c * half, half), half)
        part = dot(att_all[slot, c], wo[depth, :])
        if first:
            swaps[1].wait()
            out_acc[...] = picked(rows_ref, other_rows) + part
        else:
            out_acc[...] += part

    loads[0].wait()
    for load in loads[1:]:
        load.start()
    gather(att_all, a_send, a_recv, pieces, project)

    balanced = out_acc[...].astype(jnp.bfloat16)
    put(bal_all, b_send, b_recv, balanced)
    out_acc[...] = balanced.astype(jnp.float32)
    loads[1].wait()
    loads[2].wait()
    squares = []
    tile = 512 if hidden % 512 == 0 else 384

    def expand(slot, c, first):
        block = bal_all[slot, c].astype(jnp.float32)
        squares.append(jnp.sum(block * block, axis=1, keepdims=True))
        columns = pl.ds(pl.multiple_of(slot * width + c * half, half), half)
        scaled = (block * gain_ref[:, columns]).astype(jnp.bfloat16)
        for j in range(hidden // tile):
            part = pl.ds(j * tile, tile)
            gate = dot_t(scaled, wg[part, columns])
            up = dot_t(scaled, wu[part, columns])
            if first:
                gate_acc[:, part] = gate
                up_acc[:, part] = up
            else:
                gate_acc[:, part] += gate
                up_acc[:, part] += up

    gather(bal_all, b_send, b_recv, pieces, expand)

    scale = lax.rsqrt(sum(squares) / (width * 2 * levels) + epsilon)
    for c in range(chunks):
        part = pl.ds(c * chunk, chunk)
        gate = gate_acc[:, part] * scale
        up = up_acc[:, part] * scale
        act_all[me, c] = (gate / (1.0 + jnp.exp(-gate)) * up).astype(jnp.bfloat16)
        spread(act_all, c_send, c_recv, 0, c, 0, c >= chunks // 2)

    loads[3].wait()

    def contract(slot, c, first):
        columns = pl.ds(pl.multiple_of(slot * hidden + c * chunk, chunk), chunk)
        out_acc[...] += dot_t(act_all[slot, c], wd[:, columns])

    gather(act_all, c_send, c_recv, chunks, contract)
    out_ref[...] = out_acc[: out_ref.shape[0], :].astype(jnp.bfloat16)
    for condition, copy in sent:
        if condition is None:
            copy.wait_send()
        else:
            pl.when(condition)(copy.wait_send)


def rest(attended, layer_rows, counts, ffn_gain, out_weight, w_gate, w_up, w_down, slot_cap):
    narrow_count = lax.axis_size("narrow")
    row_count, width = attended.shape
    hidden = w_gate.shape[0]
    levels = narrow_count // 2
    chunks, pieces = hidden // 256, 2
    padded = -(-BAL // 16) * 16

    vmem = pl.BlockSpec(memory_space=pltpu.VMEM)
    hbm = pl.BlockSpec(memory_space=pl.ANY)
    chunk = hidden // chunks
    sems = pltpu.SemaphoreType.DMA
    return pl.pallas_call(
        functools.partial(rest_kernel, levels, chunks, slot_cap),
        out_shape=jax.ShapeDtypeStruct((BAL, width), jnp.bfloat16),
        in_specs=[pl.BlockSpec(memory_space=pltpu.SMEM)] + [vmem] * 3 + [hbm] * 4,
        out_specs=vmem,
        scratch_shapes=[
            pltpu.VMEM(out_weight.shape, jnp.bfloat16),
            pltpu.VMEM(w_gate.shape, jnp.bfloat16),
            pltpu.VMEM(w_up.shape, jnp.bfloat16),
            pltpu.VMEM(w_down.shape, jnp.bfloat16),
            pltpu.VMEM((row_count, width), jnp.bfloat16),
            pltpu.VMEM((row_count, width), jnp.bfloat16),
            pltpu.VMEM((narrow_count, pieces, padded, width // pieces), jnp.bfloat16),
            pltpu.VMEM((narrow_count, pieces, padded, width // pieces), jnp.bfloat16),
            pltpu.VMEM((narrow_count, chunks, padded, chunk), jnp.bfloat16),
            pltpu.VMEM((padded, hidden), jnp.float32),
            pltpu.VMEM((padded, hidden), jnp.float32),
            pltpu.VMEM((padded, width), jnp.float32),
            sems((4,)),
            sems((2,)),
            sems((2,)),
            sems((levels, pieces, 6)),
            sems((narrow_count, pieces)),
            sems((levels, pieces, 6)),
            sems((narrow_count, pieces)),
            sems((levels, chunks, 6)),
            sems((narrow_count, chunks)),
        ],
        compiler_params=pltpu.CompilerParams(
            collective_id=0, has_side_effects=True, vmem_limit_bytes=60 * 2**20
        ),
    )(
        counts,
        attended,
        layer_rows,
        ffn_gain.astype(jnp.float32).reshape(1, -1),
        out_weight,
        w_gate,
        w_up,
        w_down,
    )


def attend_kernel(heads, q_ref, cos_ref, sin_ref, k_ref, v_ref, o_ref):
    length = k_ref.shape[1] // heads
    for h in range(heads):
        lanes = slice(h * HEAD, (h + 1) * HEAD)
        spots = slice(h * length, (h + 1) * length)
        query = q_ref[0, :, lanes].astype(jnp.float32)
        turned = query * cos_ref[0] + pltpu.roll(query, HEAD // 2, 1) * sin_ref[0]
        scores = dot_t(turned.astype(jnp.bfloat16), k_ref[0, spots, :]) * HEAD ** (-0.5)
        exponent = jnp.exp(scores - jnp.max(scores, axis=1, keepdims=True))
        total = jnp.sum(exponent, axis=1, keepdims=True)
        mixture = dot(exponent.astype(jnp.bfloat16), v_ref[0, spots, :])
        o_ref[0, :, lanes] = (mixture / total).astype(jnp.bfloat16)


def attend(queries, positions, key_cache, value_cache):
    canvases, slot_cap, width = queries.shape
    heads = 2 if width % (2 * HEAD) == 0 else 1
    steps = width // (heads * HEAD)
    frequency = 500000.0 ** (-2.0 * jnp.arange(HEAD // 2, dtype=jnp.float32) / HEAD)
    angles = positions.astype(jnp.float32)[..., None] * frequency
    cosine, sine = jnp.cos(angles), jnp.sin(angles)
    cosine = jnp.concatenate([cosine, cosine], axis=-1)
    sine = jnp.concatenate([-sine, sine], axis=-1)
    table = pl.BlockSpec((1, slot_cap, HEAD), lambda c, h: (c, 0, 0))
    rows = pl.BlockSpec((1, slot_cap, heads * HEAD), lambda c, h: (c, 0, h))
    cached = pl.BlockSpec((1, key_cache.shape[1] // steps, HEAD), lambda c, h: (c, h, 0))
    return pl.pallas_call(
        functools.partial(attend_kernel, heads),
        grid=(canvases, steps),
        in_specs=[rows, table, table, cached, cached],
        out_specs=rows,
        out_shape=jax.ShapeDtypeStruct(queries.shape, jnp.bfloat16),
        compiler_params=pltpu.CompilerParams(vmem_limit_bytes=40 * 2**20),
    )(queries, cosine, sine, key_cache, value_cache)


def fits_kernel(narrow_count, groups, width, hidden):
    return narrow_count == 8 and groups == 2 and width % 256 == 0 and hidden % 768 == 0


def per_device(
    queries,
    layer_rows,
    positions,
    counts,
    key_cache,
    value_cache,
    out_weight,
    ffn_gain,
    w_gate,
    w_up,
    w_down,
):
    canvases, slot_cap, feature_share = queries.shape
    head_count = D // HEAD
    narrow_count = lax.axis_size("narrow")
    groups = lax.axis_size("wide")
    row_count = canvases * slot_cap
    if fits_kernel(narrow_count, groups, feature_share, w_gate.shape[0]):
        return rest(
            attend(queries, positions, key_cache, value_cache).reshape(row_count, feature_share),
            layer_rows.reshape(row_count, feature_share),
            counts,
            ffn_gain,
            out_weight,
            w_gate,
            w_up,
            w_down,
            slot_cap,
        )
    group_size = max(1, narrow_count // head_count)
    local_heads = max(1, head_count // narrow_count)
    bit_steps = group_size.bit_length() - 1
    device_index = lax.axis_index("narrow")
    joined = queries
    for level in range(bit_steps):
        partner = from_partner(joined, "narrow", level)
        upper_bit = device_index // 2**level % 2 == 1
        joined = jnp.where(
            upper_bit,
            jnp.concatenate([partner, joined], axis=2),
            jnp.concatenate([joined, partner], axis=2),
        )
    rotated = rotate_queries(
        joined.astype(jnp.float32).reshape(canvases, slot_cap, local_heads, HEAD), positions
    ).astype(jnp.bfloat16)
    block_rows = key_cache.shape[1] // local_heads
    key_blocks = key_cache.reshape(canvases, local_heads, block_rows, HEAD)
    value_blocks = value_cache.reshape(canvases, local_heads, block_rows, HEAD)
    scores = jnp.einsum(
        "crhd,chpd->chrp", rotated, key_blocks, preferred_element_type=jnp.float32
    ) * HEAD ** (-0.5)
    row_peak = jnp.max(scores, axis=3)
    for level in range(bit_steps):
        other_peak = from_partner(row_peak, "narrow", level)
        row_peak = jnp.maximum(row_peak, other_peak)
    exponent = jnp.exp(scores - row_peak[..., None])
    totals = jnp.sum(exponent, axis=3)
    mixture = jnp.einsum(
        "chrp,chpd->crhd",
        exponent.astype(jnp.bfloat16),
        value_blocks,
        preferred_element_type=jnp.float32,
    ).reshape(row_count, local_heads * HEAD)
    for level in reversed(range(bit_steps)):
        half_width = mixture.shape[1] // 2
        lower_part = mixture[:, :half_width]
        upper_part = mixture[:, half_width:]
        upper_bit = device_index // 2**level % 2 == 1
        outgoing = jnp.where(upper_bit, lower_part, upper_part)
        kept = jnp.where(upper_bit, upper_part, lower_part)
        arrived, arrived_totals = from_partner((outgoing, totals), "narrow", level)
        mixture = kept + arrived
        totals = totals + arrived_totals
    divisor = jnp.repeat(
        jnp.transpose(totals, (0, 2, 1)).reshape(row_count, local_heads),
        mixture.shape[1] // local_heads,
        axis=1,
    )
    attended = (mixture / divisor).astype(jnp.bfloat16)
    projected = jnp.dot(
        lax.all_gather(attended, "narrow", axis=1, tiled=True),
        out_weight,
        preferred_element_type=jnp.float32,
    )
    residual = (
        layer_rows.reshape(row_count, feature_share).astype(jnp.float32) + projected
    ).astype(jnp.bfloat16)
    outgoing_rows = route_rows(residual, counts, canvases, slot_cap, groups, BAL)
    incoming = lax.all_to_all(outgoing_rows, "wide", split_axis=0, concat_axis=0, tiled=True)
    balanced = jnp.sum(incoming.astype(jnp.float32), axis=0).astype(jnp.bfloat16)
    return feed_forward(balanced, ffn_gain, w_gate, w_up, w_down)


def solution(mesh):
    return jax.shard_map(
        per_device,
        mesh=mesh,
        in_specs=(
            P(("rep", "wide"), None, "narrow"),
            P(("rep", "wide"), None, "narrow"),
            P(("rep", "wide"), None),
            P("rep"),
            P(("rep", "wide"), "narrow", None),
            P(("rep", "wide"), "narrow", None),
            P(None, "narrow"),
            P(),
            P("narrow", None),
            P("narrow", None),
            P("narrow", None),
        ),
        out_specs=P(("rep", "wide"), "narrow"),
        check_vma=False,
    )
```
